32 devices in a mesh: img: 4 (over y, x), cap: 8 (over z, core).
Axes of the slice: x: 2, y: 2, z: 4, core: 2. Of those that a mesh axis runs over, the one named last changes fastest.
Arguments:
- images: float32 [8192, 768], P('img'), may hold values from -100 to 100
- captions: float32 [8192, 768], P('cap', 'img'), may hold values from -8 to 8
- bank: float32 [8192, 768], P('img'), may hold values from -100 to 100
Outputs:
- expected: float32 [8192, 768], P('img')
The draws below stay inside these ranges and needn't reach their ends.
All inputs are finite; a program needn't handle non-finite values.
Results may differ from the reference program's by a relative error of at most 0.0003.
Values sent between devices are 32-bit elements; how exact they have to be, the bound alone decides.
A program may use at most 448 MiB of HBM per device.

```python
import math
import jax
import jax.numpy as jnp
from jax import lax

D = 768
IMAGE_ROWS_LOCAL = 2048
BANK_DEV = 2048
NI = 8192
NC = 8192
NB = 8192
N_IMG = 4


def caption_table(key):
    first, second_input = jax.random.split(jax.random.fold_in(key, 11))
    raw = jnp.clip(jax.random.normal(first, (NC, D), jnp.float32), -4.0, 4.0)
    scale = jnp.exp(jax.random.uniform(second_input, (NC, 1), jnp.float32, math.log(0.5), math.log(2.0)))
    position = jnp.arange(NC, dtype=jnp.int32)[:, None]
    chosen = position % (NC // 8) < 4
    scale = jnp.where(chosen, jnp.float32(2.0), scale)
    return raw * scale


def embedding_rows(key, count, rising):
    first, second_input = jax.random.split(key)
    scale = jnp.exp(jax.random.uniform(second_input, (count, 1), jnp.float32, math.log(0.5), math.log(2.0)))
    if rising:
        scale = scale * jnp.exp(math.log(3.0) * jnp.arange(count, dtype=jnp.float32)[:, None] / count)
    raw = jnp.clip(jax.random.normal(first, (count, D), jnp.float32), -4.0, 4.0)
    return raw * scale


def plant(rows, key, offset):
    table = caption_table(key)
    for index in range(8):
        caption_vector = index * (NC // 8) + offset
        prior_power = 5.0 + index
        rows = rows.at[index].set(prior_power * 0.5 * (table[caption_vector] + table[caption_vector + 1]))
    return rows


def draw_captions(key, part):
    return caption_table(key)


def draw_images(key, part):
    rows = embedding_rows(jax.random.fold_in(key, 21), NI, False)
    return plant(rows, key, 0)


def draw_bank(key, part):
    rows = embedding_rows(jax.random.fold_in(key, 31), NB, True)
    return plant(rows, key, 2)


def setup_inputs(seed: int = 0) -> dict:
    key_of = jax.random.split(jax.random.key(seed), 4)
    images = draw_images(jax.random.fold_in(key_of[3], 71), 0)
    captions = draw_captions(jax.random.fold_in(key_of[3], 71), 0)
    bank = draw_bank(jax.random.fold_in(key_of[3], 71), 0)
    return dict(images=images, captions=captions, bank=bank)


exponent_divisor = 0.03


def similar(query_factor, target_factor):
    return exponent_divisor * lax.dot_general(query_factor, target_factor, (((1,), (1,)), ((), ())), precision=lax.Precision.HIGHEST, preferred_element_type=jnp.float32)


def reference(images, captions, bank):
    blocks = bank.reshape(N_IMG, BANK_DEV, D)

    def advance_caption_group(carry, block):
        peak, total = carry
        scores = similar(block, captions)
        newpeak = jnp.maximum(peak, jnp.max(scores, axis=0))
        total = total * jnp.exp(peak - newpeak) + jnp.sum(jnp.exp(scores - newpeak[None, :]), axis=0)
        return (newpeak, total), None

    start = (jnp.full((NC,), -1e30, jnp.float32), jnp.zeros((NC,), jnp.float32))
    (peak, total), ignored_argument = lax.scan(advance_caption_group, start, blocks)
    col_log = peak + jnp.log(total)

    def row_block(rows):
        logits = similar(rows, captions) - col_log[None, :]
        row_max = jnp.max(logits, axis=1, keepdims=True)
        weights = jnp.exp(logits - row_max)
        row_total = jnp.sum(weights, axis=1, keepdims=True)
        summed = jnp.dot(weights, captions, precision=lax.Precision.HIGHEST, preferred_element_type=jnp.float32)
        return summed / row_total

    result = lax.map(row_block, images.reshape(N_IMG, IMAGE_ROWS_LOCAL, D))
    return result.reshape(NI, D)
```

```python
import functools

import jax
import jax.numpy as jnp
from jax import lax
from jax.experimental import pallas as pl
from jax.experimental.pallas import tpu as pltpu
from jax.sharding import PartitionSpec as P

SCALE = 0.03
CW = 256
RB = 512
RC = 32
LAG = 2
F32 = jnp.float32
BF16 = jnp.bfloat16


def split(x):
    hi = x.astype(BF16)
    return hi, (x - hi.astype(F32)).astype(BF16)


def loop(count, body):
    def step(i, carry):
        body(i)
        return carry

    lax.fori_loop(0, count, step, 0)


def kernel(
    n, chips, images, bank, cap, out,
    rows_f, rows_h, rows_l, cap_f, cap_h, cap_l, scores, acc, red, fin,
    stats, collog, ml, factor,
    load_sem, ring_send, ring_recv, sib_send, sib_recv, st_send, st_recv, ml_send, ml_recv,
    red_send, red_recv, bc_send, bc_recv, os_send, os_recv, loc_sem,
):
    fs, cl = cap.shape
    d = n * fs
    half = images.shape[0] // 2
    k_n = cl // CW
    side = half // 2
    t_n = side // RC
    eye = (
        lax.broadcasted_iota(jnp.int32, (128, 128), 0)
        == lax.broadcasted_iota(jnp.int32, (128, 128), 1)
    )

    i = lax.axis_index("img")
    q = lax.axis_index("cap")
    core = q % 2
    z = q // 2
    sibling = q + 1 - 2 * core
    group = i * 2 + core

    def snake(p):
        return p + (p // (n // 2)) * (3 * n // 2 - 1 - 2 * p)

    pos = snake(i)
    right = snake((pos + 1) % n)
    left = snake((pos + n - 1) % n)

    def remote(src, dst, send, recv, device):
        return pltpu.make_async_remote_copy(
            src_ref=src, dst_ref=dst, send_sem=send, recv_sem=recv,
            device_id=device, device_id_type=pl.DeviceIdType.MESH,
        )

    def group_member(offset):
        g = (group + offset) % (2 * n)
        return (g // 2, z * 2 + g % 2)

    def chip_member(offset):
        return (i, ((z + offset) % chips) * 2 + core)

    loads = [
        pltpu.make_async_copy(
            ref.at[pl.ds(pl.multiple_of(core * half, half), half), :], rows_f.at[a], load_sem.at[a]
        )
        for a, ref in enumerate((bank, images))
    ]
    for copy in loads:
        copy.start()

    barrier = pltpu.get_barrier_semaphore()
    for offset in range(1, 2 * n):
        pl.semaphore_signal(barrier, inc=1, device_id=group_member(offset), device_id_type=pl.DeviceIdType.MESH)
    for offset in range(1, chips):
        pl.semaphore_signal(barrier, inc=1, device_id=chip_member(offset), device_id_type=pl.DeviceIdType.MESH)

    own_rows = pl.ds(pl.multiple_of(i * fs, fs), fs)
    for k in range(k_n):
        cap_f[core, k, own_rows, :] = cap[:, k * CW:(k + 1) * CW]
    pl.semaphore_wait(barrier, 2 * n - 1 + chips - 1)

    def ring(way, origin, h, k):
        start = snake(origin % n) * fs
        size = fs
        if h == n // 2:
            size = fs // 2
            start = start + way * size
        ref = cap_f.at[core, k, pl.ds(pl.multiple_of(start, fs // 2), size), :]
        return remote(
            ref, ref, ring_send.at[way, h - 1, k], ring_recv.at[way, h - 1, k],
            ((right, left)[way], q),
        )

    def to_sibling(j, k, c):
        rows = pl.ds(pl.multiple_of(snake((pos + j) % n) * fs, fs), fs)
        ref = cap_f.at[c, k, rows, :]
        return remote(ref, ref, sib_send.at[j, k], sib_recv.at[j, k], (i, sibling))

    def send_own(k):
        ring(0, pos, 1, k).start()
        ring(1, pos, 1, k).start()
        to_sibling(0, k, core).start()

    loop(k_n, send_own)

    def forward(k):
        for h in range(1, n // 2):
            ring(0, pos + n - h, h, k).wait_recv()
            ring(0, pos + n - h, h + 1, k).start()
            to_sibling(n - h, k, core).start()
            ring(1, pos + h, h, k).wait_recv()
            ring(1, pos + h, h + 1, k).start()
            to_sibling(h, k, core).start()

    def finish(k):
        for way in range(2):
            ring(way, pos + n // 2, n // 2, k).wait_recv()
        to_sibling(n // 2, k, core).start()

    for a in range(2):
        loads[a].wait()

        def split_rows(b, a=a):
            rows = pl.ds(pl.multiple_of(b * 128, 128), 128)
            hi, lo = split(rows_f[a, rows, :])
            rows_h[a, rows, :] = hi
            rows_l[a, rows, :] = lo

        loop(half // 128, split_rows)
        if a == 0:
            forward(0)

    def stat_copy(offset, source):
        return remote(
            stats.at[source], stats.at[source], st_send.at[offset - 1], st_recv.at[offset - 1],
            group_member(offset),
        )

    def product(a, rb, rhs):
        rows = pl.ds(pl.multiple_of(rb * RB, RB), RB)
        hi = rows_h[a, rows, :]
        lhs = jnp.concatenate([hi, hi, rows_l[a, rows, :]], axis=1)
        return SCALE * jnp.dot(lhs, rhs, preferred_element_type=F32)

    def score_chunk(v):
        k = v // 2
        w = v % 2

        @pl.when(w == 0)
        def _():
            finish(k)

        @pl.when(w == 1)
        def _():
            @pl.when(k + 1 < k_n)
            def _():
                forward(k + 1)

            for j in range(n):
                to_sibling(j, k, 1 - core).wait_recv()

        c = (core + w) % 2
        g = c * k_n + k
        hi, lo = split(cap_f[c, k])
        cap_h[g] = hi
        cap_l[g] = lo
        rhs = jnp.concatenate([cap_h[g], cap_l[g], cap_h[g]], axis=0)

        def bank_block(rb, carry):
            peak, total = carry
            s = product(0, rb, rhs)
            new = jnp.maximum(peak, jnp.max(s, axis=0, keepdims=True))
            total = total * jnp.exp(peak - new) + jnp.sum(jnp.exp(s - new), axis=0, keepdims=True)
            return new, total

        peak, total = lax.fori_loop(
            0, half // RB, bank_block, (jnp.full((1, CW), -1e30, F32), jnp.zeros((1, CW), F32))
        )
        stats[group, 0, pl.ds(g, 1), :] = peak
        stats[group, 1, pl.ds(g, 1), :] = total

        @pl.when(v == 2 * k_n - 1)
        def _():
            for offset in range(1, 2 * n):
                stat_copy(offset, group).start()

        def image_block(rb):
            scores[g, pl.ds(pl.multiple_of(rb * RB, RB), RB), :] = product(1, rb, rhs)

        loop(half // RB, image_block)

    loop(2 * k_n, score_chunk)

    for offset in range(1, 2 * n):
        stat_copy(offset, (group + 2 * n - offset) % (2 * n)).wait_recv()
    peak = stats[0, 0]
    for g in range(1, 2 * n):
        peak = jnp.maximum(peak, stats[g, 0])
    total = jnp.zeros_like(peak)
    for g in range(2 * n):
        total = total + stats[g, 1] * jnp.exp(stats[g, 0] - peak)
    collog[...] = peak + jnp.log(total)

    def weigh(b):
        rows = pl.ds(pl.multiple_of(b * 128, 128), 128)
        best = scores[0, rows, :] - collog[0:1, :]
        for g in range(1, 2 * k_n):
            best = jnp.maximum(best, scores[g, rows, :] - collog[g:g + 1, :])
        m = jnp.max(best, axis=1, keepdims=True)
        total = jnp.zeros((128, CW), F32)
        for g in range(2 * k_n):
            w = jnp.exp(scores[g, rows, :] - collog[g:g + 1, :] - m)
            scores[g, rows, :] = w
            total = total + w
        l = jnp.sum(total, axis=1, keepdims=True)
        ml[z, 0, pl.ds(b, 1), :] = jnp.sum(jnp.where(eye, m, 0.0), axis=0, keepdims=True)
        ml[z, 1, pl.ds(b, 1), :] = jnp.sum(jnp.where(eye, l, 0.0), axis=0, keepdims=True)

    loop(half // 128, weigh)

    def ml_copy(offset, source):
        return remote(
            ml.at[source], ml.at[source], ml_send.at[offset - 1], ml_recv.at[offset - 1],
            chip_member(offset),
        )

    for offset in range(1, chips):
        ml_copy(offset, z).start()

    def average(b):
        starts = [pl.multiple_of(b * 128, 128), pl.multiple_of(side + b * 128, 128)]

        def add(g):
            w = jnp.concatenate([scores[g, pl.ds(s, 128), :] for s in starts], axis=0)
            hi, lo = split(w)
            lhs = jnp.concatenate([hi, hi, lo], axis=1)
            rhs = jnp.concatenate([cap_h[g], cap_l[g], cap_h[g]], axis=1)
            part = lax.dot_general(lhs, rhs, (((1,), (1,)), ((), ())), preferred_element_type=F32)

            @pl.when(g == 0)
            def _():
                for a, s in enumerate(starts):
                    acc[pl.ds(s, 128), :] = part[a * 128:(a + 1) * 128]

            @pl.when(g > 0)
            def _():
                for a, s in enumerate(starts):
                    acc[pl.ds(s, 128), :] += part[a * 128:(a + 1) * 128]

        loop(2 * k_n, add)

        @pl.when(b == 0)
        def _():
            for offset in range(1, chips):
                ml_copy(offset, (z + chips - offset) % chips).wait_recv()
            top = ml[0, 0]
            for c in range(1, chips):
                top = jnp.maximum(top, ml[c, 0])
            whole = jnp.zeros_like(top)
            for c in range(chips):
                whole = whole + ml[c, 1] * jnp.exp(ml[c, 0] - top)
            factor[...] = jnp.exp(ml[z, 0] - top) / whole

        for a, s in enumerate(starts):
            row = factor[pl.ds(a * (side // 128) + b, 1), :]
            column = jnp.sum(jnp.where(eye, row, 0.0), axis=1, keepdims=True)
            acc[pl.ds(s, 128), :] = acc[pl.ds(s, 128), :] * column

    def chunk(way, t):
        return pl.ds(pl.multiple_of(way * side + t * RC, RC), RC)

    def place(way):
        return z if way == 0 else chips - 1 - z

    def step_device(way, by):
        zz = z + by if way == 0 else z - by
        return (i, zz * 2 + core)

    def red_copy(way, t):
        rows = chunk(way, t)
        return remote(
            acc.at[rows, :], red.at[rows, :], red_send.at[way, t], red_recv.at[way, t], step_device(way, 1)
        )

    def bc_copy(way, t, src):
        rows = chunk(way, t)
        return remote(
            src.at[rows, :], fin.at[rows, :], bc_send.at[way, t], bc_recv.at[way, t], step_device(way, -1)
        )

    def out_rows(way, t):
        return pl.ds(pl.multiple_of(core * half + way * side + t * RC, RC), RC)

    def os_copy(way, t, src):
        return remote(
            src.at[chunk(way, t), :], out.at[out_rows(way, t), :],
            os_send.at[way, t], os_recv.at[way, t], (i, sibling),
        )

    def loc_copy(way, t, src):
        return pltpu.make_async_copy(
            src.at[chunk(way, t), :], out.at[out_rows(way, t), :], loc_sem.at[way, t]
        )

    def reduce_step(s):
        for way in range(2):
            zz = place(way)
            t = s - LAG * zz

            @pl.when((t >= 0) & (t < t_n))
            def _(way=way, zz=zz, t=t):
                @pl.when(zz > 0)
                def _():
                    rows = chunk(way, t)
                    red_copy(way, t).wait_recv()
                    acc[rows, :] += red[rows, :]

                @pl.when(zz < chips - 1)
                def _():
                    red_copy(way, t).start()

                @pl.when(zz == chips - 1)
                def _():
                    if chips > 1:
                        bc_copy(way, t, acc).start()
                    os_copy(way, t, acc).start()
                    loc_copy(way, t, acc).start()

            u = s - LAG * (2 * (chips - 1) - zz)

            @pl.when((u >= 0) & (u < t_n) & (zz < chips - 1))
            def _(way=way, zz=zz, u=u):
                bc_copy(way, u, fin).wait_recv()

                @pl.when(zz > 0)
                def _():
                    bc_copy(way, u, fin).start()

                os_copy(way, u, fin).start()
                loc_copy(way, u, fin).start()

    per = 128 // RC

    def block(b):
        average(b)
        loop(per, lambda s: reduce_step(b * per + s))

    loop(t_n // per, block)
    loop(2 * LAG * (chips - 1), lambda s: reduce_step(t_n + s))

    def drain(t):
        for way in range(2):
            zz = place(way)

            @pl.when(zz < chips - 1)
            def _(way=way):
                red_copy(way, t).wait_send()

            @pl.when(zz > 0)
            def _(way=way):
                bc_copy(way, t, fin).wait_send()

            os_copy(way, t, fin).wait_send()
            loc_copy(way, t, fin).wait()
            remote(
                fin.at[chunk(way, t), :],
                out.at[pl.ds(pl.multiple_of((1 - core) * half + way * side + t * RC, RC), RC), :],
                os_send.at[way, t], os_recv.at[way, t], (i, sibling),
            ).wait_recv()

    loop(t_n, drain)

    def drain_gather(k):
        for h in range(1, n // 2 + 1):
            ring(0, pos + n - h + 1, h, k).wait_send()
            ring(1, pos + h - 1, h, k).wait_send()
        for j in range(n):
            to_sibling(j, k, core).wait_send()

    loop(k_n, drain_gather)
    for offset in range(1, 2 * n):
        stat_copy(offset, group).wait_send()
    for offset in range(1, chips):
        ml_copy(offset, z).wait_send()


def local(n, chips, images, captions, bank):
    cap = captions.T
    fs, cl = cap.shape
    d = n * fs
    rows = images.shape[0]
    half = rows // 2
    k_n = cl // CW
    t_n = half // 2 // RC
    dma = pltpu.SemaphoreType.DMA
    any_spec = pl.BlockSpec(memory_space=pl.ANY)
    return pl.pallas_call(
        functools.partial(kernel, n, chips),
        out_shape=jax.ShapeDtypeStruct((rows, d), F32),
        in_specs=[any_spec, any_spec, pl.BlockSpec(memory_space=pltpu.VMEM)],
        out_specs=any_spec,
        scratch_shapes=[
            pltpu.VMEM((2, half, d), F32),
            pltpu.VMEM((2, half, d), BF16),
            pltpu.VMEM((2, half, d), BF16),
            pltpu.VMEM((2, k_n, d, CW), F32),
            pltpu.VMEM((2 * k_n, d, CW), BF16),
            pltpu.VMEM((2 * k_n, d, CW), BF16),
            pltpu.VMEM((2 * k_n, half, CW), F32),
            pltpu.VMEM((half, d), F32),
            pltpu.VMEM((half, d), F32),
            pltpu.VMEM((half, d), F32),
            pltpu.VMEM((2 * n, 2, 2 * k_n, CW), F32),
            pltpu.VMEM((2 * k_n, CW), F32),
            pltpu.VMEM((chips, 2, half // 128, 128), F32),
            pltpu.VMEM((half // 128, 128), F32),
            dma((2,)),
            dma((2, n // 2, k_n)),
            dma((2, n // 2, k_n)),
            dma((n, k_n)),
            dma((n, k_n)),
            dma((2 * n - 1,)),
            dma((2 * n - 1,)),
            dma((chips - 1,)),
            dma((chips - 1,)),
            dma((2, t_n)),
            dma((2, t_n)),
            dma((2, t_n)),
            dma((2, t_n)),
            dma((2, t_n)),
            dma((2, t_n)),
            dma((2, t_n)),
        ],
        compiler_params=pltpu.CompilerParams(
            collective_id=0, has_side_effects=True, vmem_limit_bytes=60 * 1024 * 1024
        ),
        cost_estimate=pl.CostEstimate(
            flops=18 * half * 2 * cl * d, bytes_accessed=12 * rows * d, transcendentals=4 * half * cl
        ),
    )(images, bank, cap)


def solution(mesh):
    return jax.shard_map(
        functools.partial(local, mesh.shape["img"], mesh.shape["cap"] // 2),
        mesh=mesh,
        in_specs=(P("img", None), P("cap", "img"), P("img", None)),
        out_specs=P("img", None),
        check_vma=False,
    )
```

```python
import functools

import jax
import jax.numpy as jnp
from jax import lax
from jax.experimental import pallas as pl
from jax.experimental.pallas import tpu as pltpu
from jax.sharding import PartitionSpec as P

SCALE = 0.03
CW = 256
RB = 512
RC = 32
LAG = 2
F32 = jnp.float32
BF16 = jnp.bfloat16


def split(x):
    hi = x.astype(BF16)
    return hi, (x - hi.astype(F32)).astype(BF16)


def loop(count, body):
    def step(i, carry):
        body(i)
        return carry

    lax.fori_loop(0, count, step, 0)


def kernel(
    n, chips, images, bank, cap, out,
    rows_f, rows_h, rows_l, cap_f, cap_h, cap_l, scores, acc, red, fin,
    stats, collog, ml,
    load_sem, ring_send, ring_recv, sib_send, sib_recv, st_send, st_recv, ml_send, ml_recv,
    red_send, red_recv, bc_send, bc_recv, os_send, os_recv, loc_sem,
):
    fs, cl = cap.shape
    d = n * fs
    half = images.shape[0] // 2
    k_n = cl // CW
    side = half // 2
    t_n = side // RC
    eye = (
        lax.broadcasted_iota(jnp.int32, (128, 128), 0)
        == lax.broadcasted_iota(jnp.int32, (128, 128), 1)
    )

    i = lax.axis_index("img")
    q = lax.axis_index("cap")
    core = q % 2
    z = q // 2
    sibling = q + 1 - 2 * core
    group = i * 2 + core

    def snake(p):
        return p + (p // (n // 2)) * (3 * n // 2 - 1 - 2 * p)

    pos = snake(i)
    right = snake((pos + 1) % n)
    left = snake((pos + n - 1) % n)

    def remote(src, dst, send, recv, device):
        return pltpu.make_async_remote_copy(
            src_ref=src, dst_ref=dst, send_sem=send, recv_sem=recv,
            device_id=device, device_id_type=pl.DeviceIdType.MESH,
        )

    def group_member(offset):
        g = (group + offset) % (2 * n)
        return (g // 2, z * 2 + g % 2)

    def chip_member(offset):
        return (i, ((z + offset) % chips) * 2 + core)

    loads = [
        pltpu.make_async_copy(
            ref.at[pl.ds(pl.multiple_of(core * half, half), half), :], rows_f.at[a], load_sem.at[a]
        )
        for a, ref in enumerate((bank, images))
    ]
    for copy in loads:
        copy.start()

    barrier = pltpu.get_barrier_semaphore()
    for offset in range(1, 2 * n):
        pl.semaphore_signal(barrier, inc=1, device_id=group_member(offset), device_id_type=pl.DeviceIdType.MESH)
    for offset in range(1, chips):
        pl.semaphore_signal(barrier, inc=1, device_id=chip_member(offset), device_id_type=pl.DeviceIdType.MESH)

    own_rows = pl.ds(pl.multiple_of(i * fs, fs), fs)
    for k in range(k_n):
        cap_f[core, k, own_rows, :] = cap[:, k * CW:(k + 1) * CW]
    pl.semaphore_wait(barrier, 2 * n - 1 + chips - 1)

    def ring(way, origin, h, k):
        start = snake(origin % n) * fs
        size = fs
        if h == n // 2:
            size = fs // 2
            start = start + way * size
        ref = cap_f.at[core, k, pl.ds(pl.multiple_of(start, fs // 2), size), :]
        return remote(
            ref, ref, ring_send.at[way, h - 1, k], ring_recv.at[way, h - 1, k],
            ((right, left)[way], q),
        )

    def to_sibling(j, k, c):
        rows = pl.ds(pl.multiple_of(snake((pos + j) % n) * fs, fs), fs)
        ref = cap_f.at[c, k, rows, :]
        return remote(ref, ref, sib_send.at[j, k], sib_recv.at[j, k], (i, sibling))

    def send_own(k):
        ring(0, pos, 1, k).start()
        ring(1, pos, 1, k).start()
        to_sibling(0, k, core).start()

    loop(k_n, send_own)

    def forward(k):
        for h in range(1, n // 2):
            ring(0, pos + n - h, h, k).wait_recv()
            ring(0, pos + n - h, h + 1, k).start()
            to_sibling(n - h, k, core).start()
            ring(1, pos + h, h, k).wait_recv()
            ring(1, pos + h, h + 1, k).start()
            to_sibling(h, k, core).start()

    def finish(k):
        for way in range(2):
            ring(way, pos + n // 2, n // 2, k).wait_recv()
        to_sibling(n // 2, k, core).start()

    for a in range(2):
        loads[a].wait()

        def split_rows(b, a=a):
            rows = pl.ds(pl.multiple_of(b * 128, 128), 128)
            hi, lo = split(rows_f[a, rows, :])
            rows_h[a, rows, :] = hi
            rows_l[a, rows, :] = lo

        loop(half // 128, split_rows)
        if a == 0:
            forward(0)

    def stat_copy(offset, source):
        return remote(
            stats.at[source], stats.at[source], st_send.at[offset - 1], st_recv.at[offset - 1],
            group_member(offset),
        )

    def product(a, rb, rhs):
        rows = pl.ds(pl.multiple_of(rb * RB, RB), RB)
        hi = rows_h[a, rows, :]
        lhs = jnp.concatenate([hi, hi, rows_l[a, rows, :]], axis=1)
        return SCALE * jnp.dot(lhs, rhs, preferred_element_type=F32)

    def block_starts(b):
        return [pl.multiple_of(b * 128, 128), pl.multiple_of(side + b * 128, 128)]

    def chunk_rhs(g, axis):
        hi = cap_h[g]
        return jnp.concatenate([hi, cap_l[g], hi], axis=axis)

    def image_scores(b, g):
        parts = []
        for start in block_starts(b):
            hi = rows_h[1, pl.ds(start, 128), :]
            parts.append(jnp.concatenate([hi, hi, rows_l[1, pl.ds(start, 128), :]], axis=1))
        lhs = jnp.concatenate(parts, axis=0)
        scores[g] = SCALE * jnp.dot(lhs, chunk_rhs(g, 0), preferred_element_type=F32)

    def score_chunk(v):
        k = v // 2
        w = v % 2

        @pl.when(w == 0)
        def _():
            finish(k)

        @pl.when(w == 1)
        def _():
            @pl.when(k + 1 < k_n)
            def _():
                forward(k + 1)

            for j in range(n):
                to_sibling(j, k, 1 - core).wait_recv()

        c = (core + w) % 2
        g = c * k_n + k
        hi, lo = split(cap_f[c, k])
        cap_h[g] = hi
        cap_l[g] = lo
        rhs = chunk_rhs(g, 0)

        def bank_block(rb, carry):
            peak, total = carry
            s = product(0, rb, rhs)
            new = jnp.maximum(peak, jnp.max(s, axis=0, keepdims=True))
            total = total * jnp.exp(peak - new) + jnp.sum(jnp.exp(s - new), axis=0, keepdims=True)
            return new, total

        peak, total = lax.fori_loop(
            0, half // RB, bank_block, (jnp.full((1, CW), -1e30, F32), jnp.zeros((1, CW), F32))
        )
        stats[group, 0, pl.ds(g, 1), :] = peak
        stats[group, 1, pl.ds(g, 1), :] = total

        @pl.when(v == 2 * k_n - 1)
        def _():
            for offset in range(1, 2 * n):
                stat_copy(offset, group).start()

        image_scores(0, g)

    loop(2 * k_n, score_chunk)

    for offset in range(1, 2 * n):
        stat_copy(offset, (group + 2 * n - offset) % (2 * n)).wait_recv()
    peak = stats[0, 0]
    for g in range(1, 2 * n):
        peak = jnp.maximum(peak, stats[g, 0])
    total = jnp.zeros_like(peak)
    for g in range(2 * n):
        total = total + stats[g, 1] * jnp.exp(stats[g, 0] - peak)
    collog[...] = peak + jnp.log(total)

    def weigh(b):
        def part(a):
            rows = pl.ds(pl.multiple_of(a * 128, 128), 128)
            best = scores[0, rows, :] - collog[0:1, :]
            for g in range(1, 2 * k_n):
                best = jnp.maximum(best, scores[g, rows, :] - collog[g:g + 1, :])
            m = jnp.max(best, axis=1, keepdims=True)
            total = jnp.zeros((128, CW), F32)
            for g in range(2 * k_n):
                w = jnp.exp(scores[g, rows, :] - collog[g:g + 1, :] - m)
                scores[g, rows, :] = w
                total = total + w
            l = jnp.sum(total, axis=1, keepdims=True)
            ml[z, b, pl.ds(a, 1), :] = jnp.sum(jnp.where(eye, m, 0.0), axis=0, keepdims=True)
            ml[z, b, pl.ds(2 + a, 1), :] = jnp.sum(jnp.where(eye, l, 0.0), axis=0, keepdims=True)

        loop(2, part)
        for offset in range(1, chips):
            ml_copy(offset, z, b).start()

    def ml_copy(offset, source, b):
        return remote(
            ml.at[source, b], ml.at[source, b], ml_send.at[offset - 1, b], ml_recv.at[offset - 1, b],
            chip_member(offset),
        )

    def average(b):
        starts = block_starts(b)

        def add(g):
            hi, lo = split(scores[g])
            lhs = jnp.concatenate([hi, hi, lo], axis=1)
            part = lax.dot_general(
                lhs, chunk_rhs(g, 1), (((1,), (1,)), ((), ())), preferred_element_type=F32
            )

            @pl.when(g == 0)
            def _():
                for a, s in enumerate(starts):
                    acc[pl.ds(s, 128), :] = part[a * 128:(a + 1) * 128]

            @pl.when(g > 0)
            def _():
                for a, s in enumerate(starts):
                    acc[pl.ds(s, 128), :] += part[a * 128:(a + 1) * 128]

        loop(2 * k_n, add)

    def normalize(b):
        for offset in range(1, chips):
            ml_copy(offset, (z + chips - offset) % chips, b).wait_recv()
        top = ml[0, b, 0:2, :]
        for c in range(1, chips):
            top = jnp.maximum(top, ml[c, b, 0:2, :])
        whole = jnp.zeros_like(top)
        for c in range(chips):
            whole = whole + ml[c, b, 2:4, :] * jnp.exp(ml[c, b, 0:2, :] - top)
        factor = jnp.exp(ml[z, b, 0:2, :] - top) / whole
        for a, s in enumerate(block_starts(b)):
            column = jnp.sum(jnp.where(eye, factor[a:a + 1, :], 0.0), axis=1, keepdims=True)
            acc[pl.ds(s, 128), :] = acc[pl.ds(s, 128), :] * column

    def chunk(way, t):
        return pl.ds(pl.multiple_of(way * side + t * RC, RC), RC)

    def place(way):
        return z if way == 0 else chips - 1 - z

    def step_device(way, by):
        zz = z + by if way == 0 else z - by
        return (i, zz * 2 + core)

    def red_copy(way, t):
        rows = chunk(way, t)
        return remote(
            acc.at[rows, :], red.at[rows, :], red_send.at[way, t], red_recv.at[way, t], step_device(way, 1)
        )

    def bc_copy(way, t, src):
        rows = chunk(way, t)
        return remote(
            src.at[rows, :], fin.at[rows, :], bc_send.at[way, t], bc_recv.at[way, t], step_device(way, -1)
        )

    def out_rows(way, t):
        return pl.ds(pl.multiple_of(core * half + way * side + t * RC, RC), RC)

    def os_copy(way, t, src):
        return remote(
            src.at[chunk(way, t), :], out.at[out_rows(way, t), :],
            os_send.at[way, t], os_recv.at[way, t], (i, sibling),
        )

    def loc_copy(way, t, src):
        return pltpu.make_async_copy(
            src.at[chunk(way, t), :], out.at[out_rows(way, t), :], loc_sem.at[way, t]
        )

    def reduce_step(s):
        for way in range(2):
            zz = place(way)
            t = s - LAG * zz

            @pl.when((t >= 0) & (t < t_n))
            def _(way=way, zz=zz, t=t):
                @pl.when(zz > 0)
                def _():
                    rows = chunk(way, t)
                    red_copy(way, t).wait_recv()
                    acc[rows, :] += red[rows, :]

                @pl.when(zz < chips - 1)
                def _():
                    red_copy(way, t).start()

                @pl.when(zz == chips - 1)
                def _():
                    if chips > 1:
                        bc_copy(way, t, acc).start()
                    os_copy(way, t, acc).start()
                    loc_copy(way, t, acc).start()

            u = s - LAG * (2 * (chips - 1) - zz)

            @pl.when((u >= 0) & (u < t_n) & (zz < chips - 1))
            def _(way=way, zz=zz, u=u):
                bc_copy(way, u, fin).wait_recv()

                @pl.when(zz > 0)
                def _():
                    bc_copy(way, u, fin).start()

                os_copy(way, u, fin).start()
                loc_copy(way, u, fin).start()

    per = 128 // RC

    def phase(f):
        b = f // 4
        part = f % 4

        @pl.when(f < 4 * (side // 128))
        def _():
            @pl.when((part == 0) & (b > 0))
            def _():
                loop(2 * k_n, lambda g: image_scores(b, g))

            @pl.when(part == 1)
            def _():
                weigh(b)

            @pl.when(part == 2)
            def _():
                average(b)

            @pl.when(part == 3)
            def _():
                normalize(b)

        loop(per // 4, lambda r: reduce_step((f - 3) * (per // 4) + r))

    loop(3 + (t_n + 2 * LAG * (chips - 1)) // (per // 4), phase)

    def drain(t):
        for way in range(2):
            zz = place(way)

            @pl.when(zz < chips - 1)
            def _(way=way):
                red_copy(way, t).wait_send()

            @pl.when(zz > 0)
            def _(way=way):
                bc_copy(way, t, fin).wait_send()

            os_copy(way, t, fin).wait_send()
            loc_copy(way, t, fin).wait()
            remote(
                fin.at[chunk(way, t), :],
                out.at[pl.ds(pl.multiple_of((1 - core) * half + way * side + t * RC, RC), RC), :],
                os_send.at[way, t], os_recv.at[way, t], (i, sibling),
            ).wait_recv()

    loop(t_n, drain)

    def drain_gather(k):
        for h in range(1, n // 2 + 1):
            ring(0, pos + n - h + 1, h, k).wait_send()
            ring(1, pos + h - 1, h, k).wait_send()
        for j in range(n):
            to_sibling(j, k, core).wait_send()

    loop(k_n, drain_gather)
    for offset in range(1, 2 * n):
        stat_copy(offset, group).wait_send()
    for offset in range(1, chips):
        loop(side // 128, lambda b, offset=offset: ml_copy(offset, z, b).wait_send())


def local(n, chips, images, captions, bank):
    cap = captions.T
    fs, cl = cap.shape
    d = n * fs
    rows = images.shape[0]
    half = rows // 2
    k_n = cl // CW
    t_n = half // 2 // RC
    dma = pltpu.SemaphoreType.DMA
    any_spec = pl.BlockSpec(memory_space=pl.ANY)
    return pl.pallas_call(
        functools.partial(kernel, n, chips),
        out_shape=jax.ShapeDtypeStruct((rows, d), F32),
        in_specs=[any_spec, any_spec, pl.BlockSpec(memory_space=pltpu.VMEM)],
        out_specs=any_spec,
        scratch_shapes=[
            pltpu.VMEM((2, half, d), F32),
            pltpu.VMEM((2, half, d), BF16),
            pltpu.VMEM((2, half, d), BF16),
            pltpu.VMEM((2, k_n, d, CW), F32),
            pltpu.VMEM((2 * k_n, d, CW), BF16),
            pltpu.VMEM((2 * k_n, d, CW), BF16),
            pltpu.VMEM((2 * k_n, 256, CW), F32),
            pltpu.VMEM((half, d), F32),
            pltpu.VMEM((half, d), F32),
            pltpu.VMEM((half, d), F32),
            pltpu.VMEM((2 * n, 2, 2 * k_n, CW), F32),
            pltpu.VMEM((2 * k_n, CW), F32),
            pltpu.VMEM((chips, half // 256, 4, 128), F32),
            dma((2,)),
            dma((2, n // 2, k_n)),
            dma((2, n // 2, k_n)),
            dma((n, k_n)),
            dma((n, k_n)),
            dma((2 * n - 1,)),
            dma((2 * n - 1,)),
            dma((chips - 1, half // 256)),
            dma((chips - 1, half // 256)),
            dma((2, t_n)),
            dma((2, t_n)),
            dma((2, t_n)),
            dma((2, t_n)),
            dma((2, t_n)),
            dma((2, t_n)),
            dma((2, t_n)),
        ],
        compiler_params=pltpu.CompilerParams(
            collective_id=0, has_side_effects=True, vmem_limit_bytes=60 * 1024 * 1024
        ),
        cost_estimate=pl.CostEstimate(
            flops=18 * half * 2 * cl * d, bytes_accessed=12 * rows * d, transcendentals=4 * half * cl
        ),
    )(images, bank, cap)


def solution(mesh):
    return jax.shard_map(
        functools.partial(local, mesh.shape["img"], mesh.shape["cap"] // 2),
        mesh=mesh,
        in_specs=(P("img", None), P("cap", "img"), P("img", None)),
        out_specs=P("img", None),
        check_vma=False,
    )
```

```python
import functools

import jax
import jax.numpy as jnp
from jax import lax
from jax.experimental import pallas as pl
from jax.experimental.pallas import tpu as pltpu
from jax.sharding import PartitionSpec as P

SCALE = 0.03
CW = 256
RB = 512
RC = 16
LAG = 3
F32 = jnp.float32
BF16 = jnp.bfloat16


def split(x):
    hi = x.astype(BF16)
    return hi, (x - hi.astype(F32)).astype(BF16)


def loop(count, body):
    def step(i, carry):
        body(i)
        return carry

    lax.fori_loop(0, count, step, 0)


def kernel(
    n, chips, images, bank, cap, out,
    rows_f, rows_h, rows_l, cap_f, cap_h, cap_l, scores, acc, red,
    stats, collog, ml,
    load_sem, ring_send, ring_recv, sib_send, sib_recv, st_send, st_recv, ml_send, ml_recv,
    red_send, red_recv, bc_send, bc_recv, os_send, os_recv,
):
    fs, cl = cap.shape
    d = n * fs
    half = images.shape[0] // 2
    k_n = cl // CW
    side = half // 2
    t_n = side // RC
    eye = (
        lax.broadcasted_iota(jnp.int32, (128, 128), 0)
        == lax.broadcasted_iota(jnp.int32, (128, 128), 1)
    )

    i = lax.axis_index("img")
    q = lax.axis_index("cap")
    core = q % 2
    z = q // 2
    sibling = q + 1 - 2 * core
    group = i * 2 + core

    def snake(p):
        return p + (p // (n // 2)) * (3 * n // 2 - 1 - 2 * p)

    pos = snake(i)
    right = snake((pos + 1) % n)
    left = snake((pos + n - 1) % n)

    def remote(src, dst, send, recv, device):
        return pltpu.make_async_remote_copy(
            src_ref=src, dst_ref=dst, send_sem=send, recv_sem=recv,
            device_id=device, device_id_type=pl.DeviceIdType.MESH,
        )

    def group_member(offset):
        g = (group + offset) % (2 * n)
        return (g // 2, z * 2 + g % 2)

    def chip_member(offset):
        return (i, ((z + offset) % chips) * 2 + core)

    loads = [
        pltpu.make_async_copy(
            ref.at[pl.ds(pl.multiple_of(core * half, half), half), :], rows_f.at[a], load_sem.at[a]
        )
        for a, ref in enumerate((bank, images))
    ]
    for copy in loads:
        copy.start()

    barrier = pltpu.get_barrier_semaphore()
    for offset in range(1, 2 * n):
        pl.semaphore_signal(barrier, inc=1, device_id=group_member(offset), device_id_type=pl.DeviceIdType.MESH)
    for offset in range(1, chips):
        pl.semaphore_signal(barrier, inc=1, device_id=chip_member(offset), device_id_type=pl.DeviceIdType.MESH)

    own_rows = pl.ds(pl.multiple_of(i * fs, fs), fs)
    for k in range(k_n):
        cap_f[core, k, own_rows, :] = cap[:, k * CW:(k + 1) * CW]
    pl.semaphore_wait(barrier, 2 * n - 1 + chips - 1)

    def ring(way, origin, h, k):
        start = snake(origin % n) * fs
        size = fs
        if h == n // 2:
            size = fs // 2
            start = start + way * size
        ref = cap_f.at[core, k, pl.ds(pl.multiple_of(start, fs // 2), size), :]
        return remote(
            ref, ref, ring_send.at[way, h - 1, k], ring_recv.at[way, h - 1, k],
            ((right, left)[way], q),
        )

    def to_sibling(j, k, c):
        rows = pl.ds(pl.multiple_of(snake((pos + j) % n) * fs, fs), fs)
        ref = cap_f.at[c, k, rows, :]
        return remote(ref, ref, sib_send.at[j, k], sib_recv.at[j, k], (i, sibling))

    def send_own(k):
        ring(0, pos, 1, k).start()
        ring(1, pos, 1, k).start()
        to_sibling(0, k, core).start()

    loop(k_n, send_own)

    def forward(k):
        for h in range(1, n // 2):
            ring(0, pos + n - h, h, k).wait_recv()
            ring(0, pos + n - h, h + 1, k).start()
            to_sibling(n - h, k, core).start()
            ring(1, pos + h, h, k).wait_recv()
            ring(1, pos + h, h + 1, k).start()
            to_sibling(h, k, core).start()

    def finish(k):
        for way in range(2):
            ring(way, pos + n // 2, n // 2, k).wait_recv()
        to_sibling(n // 2, k, core).start()

    for a in range(2):
        loads[a].wait()

        def split_rows(b, a=a):
            rows = pl.ds(pl.multiple_of(b * 128, 128), 128)
            hi, lo = split(rows_f[a, rows, :])
            rows_h[a, rows, :] = hi
            rows_l[a, rows, :] = lo

        loop(half // 128, split_rows)
        if a == 0:
            forward(0)

    def stat_copy(offset, source):
        return remote(
            stats.at[source], stats.at[source], st_send.at[offset - 1], st_recv.at[offset - 1],
            group_member(offset),
        )

    def product(a, rb, rhs):
        rows = pl.ds(pl.multiple_of(rb * RB, RB), RB)
        hi = rows_h[a, rows, :]
        lhs = jnp.concatenate([hi, hi, rows_l[a, rows, :]], axis=1)
        return SCALE * jnp.dot(lhs, rhs, preferred_element_type=F32)

    def block_starts(b):
        return [pl.multiple_of(b * 128, 128), pl.multiple_of(side + b * 128, 128)]

    def chunk_rhs(g, axis):
        hi = cap_h[g]
        return jnp.concatenate([hi, cap_l[g], hi], axis=axis)

    def image_scores(b, g):
        parts = []
        for start in block_starts(b):
            hi = rows_h[1, pl.ds(start, 128), :]
            parts.append(jnp.concatenate([hi, hi, rows_l[1, pl.ds(start, 128), :]], axis=1))
        lhs = jnp.concatenate(parts, axis=0)
        scores[g] = SCALE * jnp.dot(lhs, chunk_rhs(g, 0), preferred_element_type=F32)

    def score_chunk(v):
        k = v // 2
        w = v % 2

        @pl.when(w == 0)
        def _():
            finish(k)

        @pl.when(w == 1)
        def _():
            @pl.when(k + 1 < k_n)
            def _():
                forward(k + 1)

            for j in range(n):
                to_sibling(j, k, 1 - core).wait_recv()

        c = (core + w) % 2
        g = c * k_n + k
        hi, lo = split(cap_f[c, k])
        cap_h[g] = hi
        cap_l[g] = lo
        rhs = chunk_rhs(g, 0)

        def bank_block(rb, carry):
            peak, total = carry
            s = product(0, rb, rhs)
            new = jnp.maximum(peak, jnp.max(s, axis=0, keepdims=True))
            total = total * jnp.exp(peak - new) + jnp.sum(jnp.exp(s - new), axis=0, keepdims=True)
            return new, total

        peak, total = lax.fori_loop(
            0, half // RB, bank_block, (jnp.full((1, CW), -1e30, F32), jnp.zeros((1, CW), F32))
        )
        stats[group, 0, pl.ds(g, 1), :] = peak
        stats[group, 1, pl.ds(g, 1), :] = total

        @pl.when(v == 2 * k_n - 1)
        def _():
            for offset in range(1, 2 * n):
                stat_copy(offset, group).start()

        image_scores(0, g)

    loop(2 * k_n, score_chunk)

    for offset in range(1, 2 * n):
        stat_copy(offset, (group + 2 * n - offset) % (2 * n)).wait_recv()
    peak = stats[0, 0]
    for g in range(1, 2 * n):
        peak = jnp.maximum(peak, stats[g, 0])
    total = jnp.zeros_like(peak)
    for g in range(2 * n):
        total = total + stats[g, 1] * jnp.exp(stats[g, 0] - peak)
    collog[...] = peak + jnp.log(total)

    def weigh(b):
        def part(a):
            rows = pl.ds(pl.multiple_of(a * 128, 128), 128)
            best = scores[0, rows, :] - collog[0:1, :]
            for g in range(1, 2 * k_n):
                best = jnp.maximum(best, scores[g, rows, :] - collog[g:g + 1, :])
            m = jnp.max(best, axis=1, keepdims=True)
            total = jnp.zeros((128, CW), F32)
            for g in range(2 * k_n):
                w = jnp.exp(scores[g, rows, :] - collog[g:g + 1, :] - m)
                scores[g, rows, :] = w
                total = total + w
            l = jnp.sum(total, axis=1, keepdims=True)
            ml[z, b, pl.ds(a, 1), :] = jnp.sum(jnp.where(eye, m, 0.0), axis=0, keepdims=True)
            ml[z, b, pl.ds(2 + a, 1), :] = jnp.sum(jnp.where(eye, l, 0.0), axis=0, keepdims=True)

        loop(2, part)
        for offset in range(1, chips):
            ml_copy(offset, z, b).start()

    def ml_copy(offset, source, b):
        return remote(
            ml.at[source, b], ml.at[source, b], ml_send.at[offset - 1, b], ml_recv.at[offset - 1, b],
            chip_member(offset),
        )

    def average(b):
        starts = block_starts(b)

        def add(g):
            hi, lo = split(scores[g])
            lhs = jnp.concatenate([hi, hi, lo], axis=1)
            part = lax.dot_general(
                lhs, chunk_rhs(g, 1), (((1,), (1,)), ((), ())), preferred_element_type=F32
            )

            @pl.when(g == 0)
            def _():
                for a, s in enumerate(starts):
                    acc[pl.ds(s, 128), :] = part[a * 128:(a + 1) * 128]

            @pl.when(g > 0)
            def _():
                for a, s in enumerate(starts):
                    acc[pl.ds(s, 128), :] += part[a * 128:(a + 1) * 128]

        loop(2 * k_n, add)

    def normalize(b):
        for offset in range(1, chips):
            ml_copy(offset, (z + chips - offset) % chips, b).wait_recv()
        top = ml[0, b, 0:2, :]
        for c in range(1, chips):
            top = jnp.maximum(top, ml[c, b, 0:2, :])
        whole = jnp.zeros_like(top)
        for c in range(chips):
            whole = whole + ml[c, b, 2:4, :] * jnp.exp(ml[c, b, 0:2, :] - top)
        factor = jnp.exp(ml[z, b, 0:2, :] - top) / whole
        for a, s in enumerate(block_starts(b)):
            column = jnp.sum(jnp.where(eye, factor[a:a + 1, :], 0.0), axis=1, keepdims=True)
            acc[pl.ds(s, 128), :] = acc[pl.ds(s, 128), :] * column

    def chunk(way, t):
        return pl.ds(pl.multiple_of(way * side + t * RC, RC), RC)

    def place(way):
        return z if way == 0 else chips - 1 - z

    def step_device(way, by):
        zz = z + by if way == 0 else z - by
        return (i, zz * 2 + core)

    def red_copy(way, t):
        rows = chunk(way, t)
        return remote(
            acc.at[rows, :], red.at[rows, :], red_send.at[way, t], red_recv.at[way, t], step_device(way, 1)
        )

    def out_rows(way, t, c):
        return pl.ds(pl.multiple_of(c * half + way * side + t * RC, RC), RC)

    def bc_copy(way, t):
        ref = out.at[out_rows(way, t, core), :]
        return remote(ref, ref, bc_send.at[way, t], bc_recv.at[way, t], step_device(way, -1))

    def os_copy(way, t, c):
        ref = out.at[out_rows(way, t, c), :]
        return remote(ref, ref, os_send.at[way, t], os_recv.at[way, t], (i, sibling))

    def reduce_step(s):
        for way in range(2):
            zz = place(way)
            t = s - LAG * zz

            @pl.when((t >= 0) & (t < t_n))
            def _(way=way, zz=zz, t=t):
                rows = chunk(way, t)

                @pl.when(zz > 0)
                def _():
                    red_copy(way, t).wait_recv()

                @pl.when((zz > 0) & (zz < chips - 1))
                def _():
                    acc[rows, :] += red[rows, :]

                @pl.when(zz < chips - 1)
                def _():
                    red_copy(way, t).start()

                @pl.when(zz == chips - 1)
                def _():
                    out[out_rows(way, t, core), :] = acc[rows, :] + red[rows, :]
                    bc_copy(way, t).start()
                    os_copy(way, t, core).start()

            u = s - LAG * (2 * (chips - 1) - zz)

            @pl.when((u >= 0) & (u < t_n) & (zz < chips - 1))
            def _(way=way, zz=zz, u=u):
                bc_copy(way, u).wait_recv()

                @pl.when(zz > 0)
                def _():
                    bc_copy(way, u).start()

                os_copy(way, u, core).start()

    per = 128 // RC

    def phase(f):
        b = f // 4
        part = f % 4

        @pl.when(f < 4 * (side // 128))
        def _():
            @pl.when((part == 0) & (b > 0))
            def _():
                loop(2 * k_n, lambda g: image_scores(b, g))

            @pl.when(part == 1)
            def _():
                weigh(b)

            @pl.when(part == 2)
            def _():
                average(b)

            @pl.when(part == 3)
            def _():
                normalize(b)

        loop(per // 4, lambda r: reduce_step((f - 3) * (per // 4) + r))

    loop(3 + (t_n + 2 * LAG * (chips - 1)) // (per // 4), phase)

    def drain(t):
        for way in range(2):
            zz = place(way)

            @pl.when(zz < chips - 1)
            def _(way=way):
                red_copy(way, t).wait_send()

            @pl.when(zz > 0)
            def _(way=way):
                bc_copy(way, t).wait_send()

            os_copy(way, t, core).wait_send()
            os_copy(way, t, 1 - core).wait_recv()

    loop(t_n, drain)

    def drain_gather(k):
        for h in range(1, n // 2 + 1):
            ring(0, pos + n - h + 1, h, k).wait_send()
            ring(1, pos + h - 1, h, k).wait_send()
        for j in range(n):
            to_sibling(j, k, core).wait_send()

    loop(k_n, drain_gather)
    for offset in range(1, 2 * n):
        stat_copy(offset, group).wait_send()
    for offset in range(1, chips):
        loop(side // 128, lambda b, offset=offset: ml_copy(offset, z, b).wait_send())


def local(n, chips, images, captions, bank):
    cap = captions.T
    fs, cl = cap.shape
    d = n * fs
    rows = images.shape[0]
    half = rows // 2
    k_n = cl // CW
    t_n = half // 2 // RC
    dma = pltpu.SemaphoreType.DMA
    any_spec = pl.BlockSpec(memory_space=pl.ANY)
    return pl.pallas_call(
        functools.partial(kernel, n, chips),
        out_shape=pltpu.VMEM((rows, d), F32),
        in_specs=[any_spec, any_spec, pl.BlockSpec(memory_space=pltpu.VMEM)],
        out_specs=pl.BlockSpec(memory_space=pltpu.VMEM),
        scratch_shapes=[
            pltpu.VMEM((2, half, d), F32),
            pltpu.VMEM((2, half, d), BF16),
            pltpu.VMEM((2, half, d), BF16),
            pltpu.VMEM((2, k_n, d, CW), F32),
            pltpu.VMEM((2 * k_n, d, CW), BF16),
            pltpu.VMEM((2 * k_n, d, CW), BF16),
            pltpu.VMEM((2 * k_n, 256, CW), F32),
            pltpu.VMEM((half, d), F32),
            pltpu.VMEM((half, d), F32),
            pltpu.VMEM((2 * n, 2, 2 * k_n, CW), F32),
            pltpu.VMEM((2 * k_n, CW), F32),
            pltpu.VMEM((chips, half // 256, 4, 128), F32),
            dma((2,)),
            dma((2, n // 2, k_n)),
            dma((2, n // 2, k_n)),
            dma((n, k_n)),
            dma((n, k_n)),
            dma((2 * n - 1,)),
            dma((2 * n - 1,)),
            dma((chips - 1, half // 256)),
            dma((chips - 1, half // 256)),
            dma((2, t_n)),
            dma((2, t_n)),
            dma((2, t_n)),
            dma((2, t_n)),
            dma((2, t_n)),
            dma((2, t_n)),
        ],
        compiler_params=pltpu.CompilerParams(
            collective_id=0, has_side_effects=True, vmem_limit_bytes=48 * 1024 * 1024
        ),
        cost_estimate=pl.CostEstimate(
            flops=18 * half * 2 * cl * d, bytes_accessed=12 * rows * d, transcendentals=4 * half * cl
        ),
    )(images, bank, cap)


def solution(mesh):
    return jax.shard_map(
        functools.partial(local, mesh.shape["img"], mesh.shape["cap"] // 2),
        mesh=mesh,
        in_specs=(P("img", None), P("cap", "img"), P("img", None)),
        out_specs=P("img", None),
        check_vma=False,
    )
```

```python
import functools

import jax
import jax.numpy as jnp
from jax import lax
from jax.experimental import pallas as pl
from jax.experimental.pallas import tpu as pltpu
from jax.sharding import PartitionSpec as P

SCALE = 0.03
CW = 256
RB = 512
RC = 32
LAG = 2
F32 = jnp.float32
BF16 = jnp.bfloat16


def split(x):
    hi = x.astype(BF16)
    return hi, (x - hi.astype(F32)).astype(BF16)


def loop(count, body):
    def step(i, carry):
        body(i)
        return carry

    lax.fori_loop(0, count, step, 0)


def kernel(
    n, chips, images, bank, cap, out,
    rows_f, rows_h, rows_l, cap_f, cap_h, cap_l, scores, acc, red,
    stats, collog, ml,
    load_sem, ring_send, ring_recv, sib_send, sib_recv, st_send, st_recv, ml_send, ml_recv,
    red_send, red_recv, bc_send, bc_recv, os_send, os_recv,
):
    fs, cl = cap.shape
    d = n * fs
    half = images.shape[0] // 2
    k_n = cl // CW
    side = half // 2
    t_n = side // RC
    eye = (
        lax.broadcasted_iota(jnp.int32, (128, 128), 0)
        == lax.broadcasted_iota(jnp.int32, (128, 128), 1)
    )

    i = lax.axis_index("img")
    q = lax.axis_index("cap")
    core = q % 2
    z = q // 2
    sibling = q + 1 - 2 * core
    group = i * 2 + core

    def snake(p):
        return p + (p // (n // 2)) * (3 * n // 2 - 1 - 2 * p)

    pos = snake(i)
    right = snake((pos + 1) % n)
    left = snake((pos + n - 1) % n)

    def remote(src, dst, send, recv, device):
        return pltpu.make_async_remote_copy(
            src_ref=src, dst_ref=dst, send_sem=send, recv_sem=recv,
            device_id=device, device_id_type=pl.DeviceIdType.MESH,
        )

    def group_member(offset):
        g = (group + offset) % (2 * n)
        return (g // 2, z * 2 + g % 2)

    def chip_member(offset):
        return (i, ((z + offset) % chips) * 2 + core)

    loads = [
        pltpu.make_async_copy(
            ref.at[pl.ds(pl.multiple_of(core * half, half), half), :], rows_f.at[a], load_sem.at[a]
        )
        for a, ref in enumerate((bank, images))
    ]
    for copy in loads:
        copy.start()

    barrier = pltpu.get_barrier_semaphore()
    for offset in range(1, 2 * n):
        pl.semaphore_signal(barrier, inc=1, device_id=group_member(offset), device_id_type=pl.DeviceIdType.MESH)
    for offset in range(1, chips):
        pl.semaphore_signal(barrier, inc=1, device_id=chip_member(offset), device_id_type=pl.DeviceIdType.MESH)

    own_rows = pl.ds(pl.multiple_of(i * fs, fs), fs)
    for k in range(k_n):
        cap_f[core, k, own_rows, :] = cap[:, k * CW:(k + 1) * CW]
    pl.semaphore_wait(barrier, 2 * n - 1 + chips - 1)

    def ring(way, origin, h, k):
        start = snake(origin % n) * fs
        size = fs
        if h == n // 2:
            size = fs // 2
            start = start + way * size
        ref = cap_f.at[core, k, pl.ds(pl.multiple_of(start, fs // 2), size), :]
        return remote(
            ref, ref, ring_send.at[way, h - 1, k], ring_recv.at[way, h - 1, k],
            ((right, left)[way], q),
        )

    def to_sibling(j, k, c):
        rows = pl.ds(pl.multiple_of(snake((pos + j) % n) * fs, fs), fs)
        ref = cap_f.at[c, k, rows, :]
        return remote(ref, ref, sib_send.at[j, k], sib_recv.at[j, k], (i, sibling))

    def send_own(k):
        ring(0, pos, 1, k).start()
        ring(1, pos, 1, k).start()
        to_sibling(0, k, core).start()

    loop(min(2, k_n), send_own)

    def forward(k):
        for h in range(1, n // 2):
            ring(0, pos + n - h, h, k).wait_recv()
            ring(0, pos + n - h, h + 1, k).start()
            to_sibling(n - h, k, core).start()
            ring(1, pos + h, h, k).wait_recv()
            ring(1, pos + h, h + 1, k).start()
            to_sibling(h, k, core).start()

    def finish(k):
        for way in range(2):
            ring(way, pos + n // 2, n // 2, k).wait_recv()
        to_sibling(n // 2, k, core).start()

    for a in range(2):
        loads[a].wait()

        def split_rows(b, a=a):
            rows = pl.ds(pl.multiple_of(b * 128, 128), 128)
            hi, lo = split(rows_f[a, rows, :])
            rows_h[a, rows, :] = hi
            rows_l[a, rows, :] = lo

        loop(half // 128, split_rows)
        if a < k_n:
            forward(a)
        if a + 2 < k_n and a == 0:
            send_own(2)

    def stat_copy(offset, source):
        return remote(
            stats.at[source], stats.at[source], st_send.at[offset - 1], st_recv.at[offset - 1],
            group_member(offset),
        )

    def product(a, rb, rhs):
        rows = pl.ds(pl.multiple_of(rb * RB, RB), RB)
        hi = rows_h[a, rows, :]
        lhs = jnp.concatenate([hi, hi, rows_l[a, rows, :]], axis=1)
        return SCALE * jnp.dot(lhs, rhs, preferred_element_type=F32)

    def block_starts(b):
        return [pl.multiple_of(b * 128, 128), pl.multiple_of(side + b * 128, 128)]

    def chunk_rhs(g, axis):
        hi = cap_h[g]
        return jnp.concatenate([hi, cap_l[g], hi], axis=axis)

    def image_scores(b, g):
        parts = []
        for start in block_starts(b):
            hi = rows_h[1, pl.ds(start, 128), :]
            parts.append(jnp.concatenate([hi, hi, rows_l[1, pl.ds(start, 128), :]], axis=1))
        lhs = jnp.concatenate(parts, axis=0)
        scores[g] = SCALE * jnp.dot(lhs, chunk_rhs(g, 0), preferred_element_type=F32)

    def score_chunk(v):
        k = v // 2
        w = v % 2

        @pl.when(w == 0)
        def _():
            finish(k)

        @pl.when(w == 1)
        def _():
            @pl.when(k + 3 < k_n)
            def _():
                send_own(k + 3)

            @pl.when(k + 2 < k_n)
            def _():
                forward(k + 2)

            for j in range(n):
                to_sibling(j, k, 1 - core).wait_recv()

        c = (core + w) % 2
        g = c * k_n + k
        hi, lo = split(cap_f[c, k])
        cap_h[g] = hi
        cap_l[g] = lo
        rhs = chunk_rhs(g, 0)

        def bank_block(rb, carry):
            peak, total = carry
            s = product(0, rb, rhs)
            new = jnp.maximum(peak, jnp.max(s, axis=0, keepdims=True))
            total = total * jnp.exp(peak - new) + jnp.sum(jnp.exp(s - new), axis=0, keepdims=True)
            return new, total

        peak, total = lax.fori_loop(
            0, half // RB, bank_block, (jnp.full((1, CW), -1e30, F32), jnp.zeros((1, CW), F32))
        )
        stats[group, 0, pl.ds(g, 1), :] = peak
        stats[group, 1, pl.ds(g, 1), :] = total

        @pl.when(v == 2 * k_n - 1)
        def _():
            for offset in range(1, 2 * n):
                stat_copy(offset, group).start()

        image_scores(0, g)

    loop(2 * k_n, score_chunk)

    for offset in range(1, 2 * n):
        stat_copy(offset, (group + 2 * n - offset) % (2 * n)).wait_recv()
    peak = stats[0, 0]
    for g in range(1, 2 * n):
        peak = jnp.maximum(peak, stats[g, 0])
    total = jnp.zeros_like(peak)
    for g in range(2 * n):
        total = total + stats[g, 1] * jnp.exp(stats[g, 0] - peak)
    collog[...] = peak + jnp.log(total)

    def weigh(b):
        def part(a):
            rows = pl.ds(pl.multiple_of(a * 128, 128), 128)
            best = scores[0, rows, :] - collog[0:1, :]
            for g in range(1, 2 * k_n):
                best = jnp.maximum(best, scores[g, rows, :] - collog[g:g + 1, :])
            m = jnp.max(best, axis=1, keepdims=True)
            total = jnp.zeros((128, CW), F32)
            for g in range(2 * k_n):
                w = jnp.exp(scores[g, rows, :] - collog[g:g + 1, :] - m)
                scores[g, rows, :] = w
                total = total + w
            l = jnp.sum(total, axis=1, keepdims=True)
            ml[z, b, pl.ds(a, 1), :] = jnp.sum(jnp.where(eye, m, 0.0), axis=0, keepdims=True)
            ml[z, b, pl.ds(2 + a, 1), :] = jnp.sum(jnp.where(eye, l, 0.0), axis=0, keepdims=True)

        loop(2, part)
        for offset in range(1, chips):
            ml_copy(offset, z, b).start()

    def ml_copy(offset, source, b):
        return remote(
            ml.at[source, b], ml.at[source, b], ml_send.at[offset - 1, b], ml_recv.at[offset - 1, b],
            chip_member(offset),
        )

    def average(b):
        starts = block_starts(b)

        def add(g):
            hi, lo = split(scores[g])
            lhs = jnp.concatenate([hi, hi, lo], axis=1)
            part = lax.dot_general(
                lhs, chunk_rhs(g, 1), (((1,), (1,)), ((), ())), preferred_element_type=F32
            )

            @pl.when(g == 0)
            def _():
                for a, s in enumerate(starts):
                    acc[pl.ds(s, 128), :] = part[a * 128:(a + 1) * 128]

            @pl.when(g > 0)
            def _():
                for a, s in enumerate(starts):
                    acc[pl.ds(s, 128), :] += part[a * 128:(a + 1) * 128]

        loop(2 * k_n, add)

    def normalize(b):
        for offset in range(1, chips):
            ml_copy(offset, (z + chips - offset) % chips, b).wait_recv()
        top = ml[0, b, 0:2, :]
        for c in range(1, chips):
            top = jnp.maximum(top, ml[c, b, 0:2, :])
        whole = jnp.zeros_like(top)
        for c in range(chips):
            whole = whole + ml[c, b, 2:4, :] * jnp.exp(ml[c, b, 0:2, :] - top)
        factor = jnp.exp(ml[z, b, 0:2, :] - top) / whole
        for a, s in enumerate(block_starts(b)):
            column = jnp.sum(jnp.where(eye, factor[a:a + 1, :], 0.0), axis=1, keepdims=True)
            acc[pl.ds(s, 128), :] = acc[pl.ds(s, 128), :] * column

    def chunk(way, t):
        return pl.ds(pl.multiple_of(way * side + t * RC, RC), RC)

    def place(way):
        return z if way == 0 else chips - 1 - z

    def step_device(way, by):
        zz = z + by if way == 0 else z - by
        return (i, zz * 2 + core)

    def red_copy(way, t):
        rows = chunk(way, t)
        return remote(
            acc.at[rows, :], red.at[rows, :], red_send.at[way, t], red_recv.at[way, t], step_device(way, 1)
        )

    def out_rows(way, t, c):
        return pl.ds(pl.multiple_of(c * half + way * side + t * RC, RC), RC)

    def bc_copy(way, t):
        ref = out.at[out_rows(way, t, core), :]
        return remote(ref, ref, bc_send.at[way, t], bc_recv.at[way, t], step_device(way, -1))

    def os_copy(way, t, c):
        ref = out.at[out_rows(way, t, c), :]
        return remote(ref, ref, os_send.at[way, t], os_recv.at[way, t], (i, sibling))

    def reduce_step(s):
        for way in range(2):
            zz = place(way)
            t = s - LAG * zz

            @pl.when((t >= 0) & (t < t_n))
            def _(way=way, zz=zz, t=t):
                rows = chunk(way, t)

                @pl.when(zz > 0)
                def _():
                    red_copy(way, t).wait_recv()

                @pl.when((zz > 0) & (zz < chips - 1))
                def _():
                    acc[rows, :] += red[rows, :]

                @pl.when(zz < chips - 1)
                def _():
                    red_copy(way, t).start()

                @pl.when(zz == chips - 1)
                def _():
                    out[out_rows(way, t, core), :] = acc[rows, :] + red[rows, :]
                    bc_copy(way, t).start()
                    os_copy(way, t, core).start()

            u = s - LAG * (2 * (chips - 1) - zz)

            @pl.when((u >= 0) & (u < t_n) & (zz < chips - 1))
            def _(way=way, zz=zz, u=u):
                bc_copy(way, u).wait_recv()

                @pl.when(zz > 0)
                def _():
                    bc_copy(way, u).start()

                os_copy(way, u, core).start()

    per = 128 // RC

    def phase(f):
        b = f // 4
        part = f % 4

        @pl.when(f < 4 * (side // 128))
        def _():
            @pl.when((part == 0) & (b > 0))
            def _():
                loop(2 * k_n, lambda g: image_scores(b, g))

            @pl.when(part == 1)
            def _():
                weigh(b)

            @pl.when(part == 2)
            def _():
                average(b)

            @pl.when(part == 3)
            def _():
                normalize(b)

        loop(per // 4, lambda r: reduce_step((f - 3) * (per // 4) + r))

    loop(3 + (t_n + 2 * LAG * (chips - 1)) // (per // 4), phase)

    def drain(t):
        for way in range(2):
            zz = place(way)

            @pl.when(zz < chips - 1)
            def _(way=way):
                red_copy(way, t).wait_send()

            @pl.when(zz > 0)
            def _(way=way):
                bc_copy(way, t).wait_send()

            os_copy(way, t, core).wait_send()
            os_copy(way, t, 1 - core).wait_recv()

    loop(t_n, drain)

    def drain_gather(k):
        for h in range(1, n // 2 + 1):
            ring(0, pos + n - h + 1, h, k).wait_send()
            ring(1, pos + h - 1, h, k).wait_send()
        for j in range(n):
            to_sibling(j, k, core).wait_send()

    loop(k_n, drain_gather)
    for offset in range(1, 2 * n):
        stat_copy(offset, group).wait_send()
    for offset in range(1, chips):
        loop(side // 128, lambda b, offset=offset: ml_copy(offset, z, b).wait_send())


def local(n, chips, images, captions, bank):
    cap = captions.T
    fs, cl = cap.shape
    d = n * fs
    rows = images.shape[0]
    half = rows // 2
    k_n = cl // CW
    t_n = half // 2 // RC
    dma = pltpu.SemaphoreType.DMA
    any_spec = pl.BlockSpec(memory_space=pl.ANY)
    return pl.pallas_call(
        functools.partial(kernel, n, chips),
        out_shape=pltpu.VMEM((rows, d), F32),
        in_specs=[any_spec, any_spec, pl.BlockSpec(memory_space=pltpu.VMEM)],
        out_specs=pl.BlockSpec(memory_space=pltpu.VMEM),
        scratch_shapes=[
            pltpu.VMEM((2, half, d), F32),
            pltpu.VMEM((2, half, d), BF16),
            pltpu.VMEM((2, half, d), BF16),
            pltpu.VMEM((2, k_n, d, CW), F32),
            pltpu.VMEM((2 * k_n, d, CW), BF16),
            pltpu.VMEM((2 * k_n, d, CW), BF16),
            pltpu.VMEM((2 * k_n, 256, CW), F32),
            pltpu.VMEM((half, d), F32),
            pltpu.VMEM((half, d), F32),
            pltpu.VMEM((2 * n, 2, 2 * k_n, CW), F32),
            pltpu.VMEM((2 * k_n, CW), F32),
            pltpu.VMEM((chips, half // 256, 4, 128), F32),
            dma((2,)),
            dma((2, n // 2, k_n)),
            dma((2, n // 2, k_n)),
            dma((n, k_n)),
            dma((n, k_n)),
            dma((2 * n - 1,)),
            dma((2 * n - 1,)),
            dma((chips - 1, half // 256)),
            dma((chips - 1, half // 256)),
            dma((2, t_n)),
            dma((2, t_n)),
            dma((2, t_n)),
            dma((2, t_n)),
            dma((2, t_n)),
            dma((2, t_n)),
        ],
        compiler_params=pltpu.CompilerParams(
            collective_id=0, has_side_effects=True, vmem_limit_bytes=48 * 1024 * 1024
        ),
        cost_estimate=pl.CostEstimate(
            flops=18 * half * 2 * cl * d, bytes_accessed=12 * rows * d, transcendentals=4 * half * cl
        ),
    )(images, bank, cap)


def solution(mesh):
    return jax.shard_map(
        functools.partial(local, mesh.shape["img"], mesh.shape["cap"] // 2),
        mesh=mesh,
        in_specs=(P("img", None), P("cap", "img"), P("img", None)),
        out_specs=P("img", None),
        check_vma=False,
    )
```
